32 devices in a mesh: dp: 8 (over z, x), seq: 4 (over y, core).
Axes of the slice: x: 2, y: 2, z: 4, core: 2. Of those that a mesh axis runs over, the one named last changes fastest.
Arguments:
- tokens: bfloat16 [4096, 1152], P(('dp', 'seq')), may hold values from -6 to 6
- gain: float32 [1152], replicated, may hold values from 0.5 to 1.5
- w_qkv: bfloat16 [1152, 3456], replicated, may hold values from -0.1875 to 0.1875
- w_out: bfloat16 [1152, 1152], replicated, may hold values from -0.1875 to 0.1875
- dest: int32 [4096, 1], P(('dp', 'seq')), may hold values from 0 to 7; in each aligned block of 128 rows (0 to 127, 128 to 255, ...) at most 32 rows name the same one
- track: int32 [4096], P(('dp', 'seq')), may hold values from 0 to 3
- cotangent: bfloat16 [4096, 1152], P(('dp', 'seq')), may hold values from -6 to 6
Outputs:
- output: bfloat16 [4096, 1152], P(('dp', 'seq'))
- grad_tokens: bfloat16 [4096, 1152], P(('dp', 'seq'))
The draws below stay inside these ranges and needn't reach their ends.
Inputs may be any that keep to these rules, and one draw needn't show every extreme that they name: `dest`: among the 128 tokens of one device, at most 32 name any one group, a bound that some block reaches.
All inputs are finite; a program needn't handle non-finite values.
Results may differ from the reference program's by a relative error of at most 0.0051.
Values may be sent and summed in bfloat16 or wider, within the bound.
A program may use at most 128 MiB of HBM per device.

```python
import math
import jax
import jax.numpy as jnp
import numpy as np
from jax import lax

D = 1152
HEADS = 16
HEAD = 72
TOK_DEV = 128
TRACKS = 4
CAP = 32
ROWS = 4096
N_DP = 8
N_SEQ = 4


def plant(drawn, key, least, high):
    place = [jax.random.randint(jax.random.fold_in(key, axis), (), 0, length) for axis, length in enumerate(drawn.shape)]
    main_axis = drawn.shape.index(max(drawn.shape))
    neighbour = place[:main_axis] + [(place[main_axis] + 1) % drawn.shape[main_axis]] + place[main_axis + 1:]
    return drawn.at[tuple(place)].set(least).at[tuple(neighbour)].set(high)


def block_scale(rng, shape, cuts, least, largest):
    def one(axis_at, blocks):
        draws = jax.random.uniform(jax.random.fold_in(jax.random.fold_in(rng, 6), axis_at), (blocks,), jnp.float32, least / len(cuts), largest / len(cuts))
        return jnp.repeat(jnp.exp(draws), shape[axis_at] // blocks).reshape((-1,) + (1,) * (len(shape) - axis_at - 1))

    level = one(*cuts[0])
    for cut in cuts[1:]:
        level = level * one(*cut)
    return level


def deal_out(rng, own, number, rows, count, top, reach, lean):
    sequence = jax.random.permutation(rng, count)
    crowded, ordinary = load_shares(count, rows * top, reach, lean, True), load_shares(count, rows * top, reach, lean, False)
    places = jnp.arange(count)

    def named(tallies, turn):
        used = int((tallies > 0).sum())
        fixed = max(1, used // 4)
        moved = fixed + (places - fixed + turn * (used - fixed)) % max(1, count - fixed)
        return jnp.zeros((count,), jnp.int32).at[sequence[jnp.where(places < fixed, places, moved)]].set(jnp.asarray(tallies, jnp.int32))

    tallies = jnp.where(number % 4 == 0, named(crowded, number // 4), named(ordinary, number - number // 4 - 1))
    mixed = jax.random.permutation(jax.random.fold_in(own, 3), count)
    donor, sink = mixed[0:count // 2 * 2:2], mixed[1:count // 2 * 2:2]
    margin = jnp.minimum(tallies[donor] - 1, reach - tallies[sink]) // 2
    margin = jnp.where((donor == sequence[0]) | (sink == sequence[0]) | (tallies[sink] == 0), 0, jnp.maximum(margin, 0))
    moved = jax.random.randint(jax.random.fold_in(own, 4), (count // 2,), 0, 1 << 20) % (margin + 1)
    tallies = tallies.at[donor].add(-moved).at[sink].add(moved)
    items = jnp.searchsorted(jnp.cumsum(tallies), jnp.arange(rows * top), side="right").astype(jnp.int32)
    table = items.reshape(top, rows).T
    table = table[jax.random.permutation(jax.random.fold_in(own, 1), rows)]
    turn = jax.random.randint(jax.random.fold_in(own, 2), (rows, 1), 0, top)
    return jnp.take_along_axis(table, (jnp.arange(top)[None, :] + turn) % top, axis=1)


def load_shares(count, total, most, skew, full):
    loads = [(1 << 20) // math.isqrt(standing ** skew) + 1 for standing in range(1, count + 1)]
    largest = most if full else min(most, max(-(-total // count), total * loads[0] // sum(loads)))
    least = 1 if total - largest >= count - 1 else 0
    counts, surplus = [largest] + [least] * (count - 1), total - largest - least * (count - 1)
    while surplus > 0:
        free = [i for i in range(1, count) if counts[i] < largest] or [i for i in range(1, count) if counts[i] < most]
        whole, left = sum([loads[i] for i in free]), surplus
        for i in free:
            more = min(most - counts[i], max(1, left * loads[i] // whole), surplus)
            counts[i] = counts[i] + more
            surplus = surplus - more
    return np.array(counts)


def noise(rng, dims, scale, most, pieces=(), kind=jnp.bfloat16):
    values = jax.random.normal(rng, dims, jnp.float32) * scale
    if len(pieces) > 0:
        values = block_scale(rng, dims, pieces, -0.22, 0.18) * values
    return jnp.clip(values, min=-most, max=most).astype(kind)


def setup_inputs(seed: int = 0) -> dict:
    splits = jax.random.split(jax.random.key(seed), 8)
    tokens = noise(splits[0], (ROWS, D), 1.0, 6.0, ((0, 32),))
    gain = jnp.clip(1.0 + 0.1 * jax.random.normal(splits[1], (D,), jnp.float32), 0.5, 1.5)
    w_qkv = noise(splits[2], (D, 3 * D), D ** -0.5, 0.1875)
    w_out = noise(splits[3], (D, D), D ** -0.5, 0.1875)
    dest_keys = jax.random.split(jax.random.fold_in(splits[4], 1), ROWS // TOK_DEV)
    dest_turns = jax.random.permutation(jax.random.fold_in(splits[4], 3), ROWS // TOK_DEV)
    dest = jax.vmap(lambda own, number: deal_out(jax.random.fold_in(splits[4], 2), own, number, TOK_DEV, N_DP, 1, CAP, 2))(dest_keys, dest_turns).reshape((ROWS, 1))
    track = plant(jax.random.randint(splits[5], (ROWS,), 0, TRACKS), jax.random.fold_in(splits[5], 1), 0, TRACKS - 1).astype(jnp.int32)
    cotangent = noise(splits[6], (ROWS, D), 1.0, 6.0, ((0, 32),))
    return {"tokens": tokens, "gain": gain, "w_qkv": w_qkv, "w_out": w_out, "dest": dest, "track": track, "cotangent": cotangent}


def normalize(rows, gain):
    mean = lax.optimization_barrier(jnp.mean(rows, axis=1, keepdims=True))
    centred = rows - mean
    var = lax.optimization_barrier(jnp.mean(centred * centred, axis=1, keepdims=True))
    return centred * lax.rsqrt(var + 1e-06) * gain[None, :]

def masked_scores(query, keys, qtrack, ktrack):
    scores = jnp.einsum('qhe,khe->hqk', query.astype(jnp.float32), keys.astype(jnp.float32))
    scores = scores * HEAD ** (-0.5)
    match = qtrack[:, None] == ktrack[None, :]
    return jnp.where(match[None], scores, -1e+30)

def attend(query, keys, values, qtrack, ktrack):
    scores = masked_scores(query, keys, qtrack, ktrack)
    top = lax.optimization_barrier(jnp.max(scores, axis=2, keepdims=True))
    expo = jnp.exp(scores - top)
    total = lax.optimization_barrier(jnp.sum(expo, axis=2, keepdims=True))
    weights = (expo / total).astype(jnp.bfloat16)
    result = jnp.einsum('hqk,khe->qhe', weights.astype(jnp.float32), values.astype(jnp.float32))
    return (result.astype(jnp.bfloat16), (top + jnp.log(total))[:, :, 0])

def attend_back(query, keys, values, result, grad_res, lse, qtrack, ktrack):
    scores = masked_scores(query, keys, qtrack, ktrack)
    prob = jnp.exp(scores - lse[:, :, None])
    weights = prob.astype(jnp.bfloat16).astype(jnp.float32)
    grad_f = grad_res.astype(jnp.float32)
    dprob = jnp.einsum('qhe,khe->hqk', grad_f, values.astype(jnp.float32))
    delta = jnp.einsum('qhe,qhe->hq', grad_f, result.astype(jnp.float32))
    dscore = (prob * (dprob - delta[:, :, None])).astype(jnp.bfloat16).astype(jnp.float32)
    scale = HEAD ** (-0.5)
    grad_q = jnp.einsum('hqk,khe->qhe', dscore, keys.astype(jnp.float32)) * scale
    grad_k = jnp.einsum('hqk,qhe->khe', dscore, query.astype(jnp.float32)) * scale
    grad_v = jnp.einsum('hqk,qhe->khe', weights, grad_f)
    return (grad_q, grad_k, grad_v)

def reference(tokens, gain, w_qkv, w_out, dest, track, cotangent):
    devices = N_DP * N_SEQ
    span = N_DP * CAP
    gsize = N_SEQ * span
    clip_group = dest[:, 0].astype(jnp.int32)
    blocks = clip_group.reshape(devices, TOK_DEV)
    onehot = (blocks[:, :, None] == jnp.arange(N_DP, dtype=jnp.int32)[None, None, :]).astype(jnp.int32)
    rank = lax.optimization_barrier(jnp.sum(jnp.cumsum(onehot, axis=1) * onehot, axis=2)) - 1
    device_ids = jnp.arange(devices, dtype=jnp.int32)[:, None]
    plan_slot = (device_ids % N_SEQ * span + device_ids // N_SEQ * CAP + rank).reshape(-1).astype(jnp.int32)
    rows_f = tokens.astype(jnp.float32)
    normed, ln_back = jax.vjp(lambda value: normalize(value, gain), rows_f)
    qkv = jnp.dot(normed.astype(jnp.bfloat16), w_qkv, preferred_element_type=jnp.float32).astype(jnp.bfloat16)
    query_buffer = jnp.zeros((N_DP, gsize, 3 * D), jnp.bfloat16).at[clip_group, plan_slot].set(qkv)
    token_buffer = jnp.full((N_DP, gsize), -1, jnp.int32).at[clip_group, plan_slot].set(track.astype(jnp.int32))

    def forward(items):
        buf, tracks = items
        split = buf.reshape(gsize, 3, HEADS, HEAD)
        result, lse = attend(split[:, 0], split[:, 1], split[:, 2], tracks, tracks)
        return (result.reshape(gsize, D), lse)
    attention_buffer, log_sum_exponents = lax.map(forward, (query_buffer, token_buffer))
    attended = attention_buffer[clip_group, plan_slot]
    output = (rows_f + jnp.dot(attended, w_out, preferred_element_type=jnp.float32)).astype(jnp.bfloat16)
    grad_att = jnp.dot(cotangent, w_out.T, preferred_element_type=jnp.float32).astype(jnp.bfloat16)
    delta_buffer = jnp.zeros((N_DP, gsize, D), jnp.bfloat16).at[clip_group, plan_slot].set(grad_att)

    def backward_sweep(items):
        buf, tracks, abuf_g, lse, dbuf_g = items
        split = buf.reshape(gsize, 3, HEADS, HEAD)
        grads = attend_back(split[:, 0], split[:, 1], split[:, 2], abuf_g.reshape(gsize, HEADS, HEAD), dbuf_g.reshape(gsize, HEADS, HEAD), lse, tracks, tracks)
        return jnp.stack(grads, axis=1).astype(jnp.bfloat16).reshape(gsize, 3 * D)
    gradient_buffer = lax.map(backward_sweep, (query_buffer, token_buffer, attention_buffer, log_sum_exponents, delta_buffer))
    query_key_value_gradient = gradient_buffer[clip_group, plan_slot]
    grad_normed = jnp.dot(query_key_value_gradient, w_qkv.T, preferred_element_type=jnp.float32)
    grad_tokens = (cotangent.astype(jnp.float32) + ln_back(grad_normed)[0]).astype(jnp.bfloat16)
    return (output, grad_tokens)
```

```python
import functools

import jax
import jax.numpy as jnp
from jax import lax
from jax.experimental import pallas as pl
from jax.experimental.pallas import tpu as pltpu
from jax.sharding import PartitionSpec as P

HEADS = 16
HEAD = 72
LANES = 128
SCALE = HEAD ** (-0.5)
MESH = pl.DeviceIdType.MESH
VMEM = pl.BlockSpec(memory_space=pltpu.VMEM)
BF = jnp.bfloat16
F32 = jnp.float32
NT = (((1,), (1,)), ((), ()))
TN = (((0,), (0,)), ((), ()))


def dot(a, b, dims=(((1,), (0,)), ((), ()))):
    return lax.dot_general(a, b, dims, preferred_element_type=F32)


def flip(index, mask):
    bit = 1
    out = index
    while bit <= mask:
        if mask & bit:
            out = out + bit * (1 - 2 * ((index // bit) % 2))
        bit *= 2
    return out


def greet(partners):
    barrier = pltpu.get_barrier_semaphore()
    for device in partners:
        pl.semaphore_signal(barrier, inc=1, device_id=device, device_id_type=MESH)
    pl.semaphore_wait(barrier, len(partners))


def partners_of(groups):
    me, part = lax.axis_index("dp"), lax.axis_index("seq")
    far = [(flip(me, o), part) for o in range(groups)]
    return far, (me, flip(part, 1)), (me, flip(part, 2)), me


def gather_kernel(groups, width, pay, wqkv, wout, qkv, gatt, tracks, held, s_dp, r_dp, s_y, r_y, s_c, r_c):
    far, sibling, across, me = partners_of(groups)
    greet(far[1:] + [sibling, across])
    cap = pay.shape[1]

    def remote(src, dst, send, recv, device):
        return pltpu.make_async_remote_copy(
            src_ref=src, dst_ref=dst, send_sem=send, recv_sem=recv, device_id=device, device_id_type=MESH
        )

    first = [
        remote(pay.at[far[o][0]], held.at[o, 0], s_dp.at[o], r_dp.at[o], far[o]) if o else None
        for o in range(groups)
    ]
    half = groups // 2
    for o in list(range(half, groups)) + list(range(1, half)):
        first[o].start()
    held[0, 0] = pay[me]
    to_y = [remote(held.at[o, 0], held.at[o, 2], s_y.at[o], r_y.at[o], across) for o in range(groups)]
    to_c = [remote(held.at[o, 0], held.at[o, 1], s_c.at[o, 0], r_c.at[o, 0], sibling) for o in range(groups)]
    to_d = [remote(held.at[o, 2], held.at[o, 3], s_c.at[o, 1], r_c.at[o, 1], sibling) for o in range(groups)]
    for step in range(groups + 2):
        if step < groups:
            if step:
                first[step].wait_recv()
            to_y[step].start()
            to_c[step].start()
        if 1 <= step <= groups:
            to_y[step - 1].wait_recv()
            to_d[step - 1].start()
        if step >= 2:
            o = step - 2
            to_c[o].wait_recv()
            to_d[o].wait_recv()
            block = held[o].reshape(4 * cap, held.shape[3])
            rows = pl.ds(o * 4 * cap, 4 * cap)
            qkv[rows, :] = dot(block[:, :width], wqkv[...]).astype(BF)
            gatt[rows, :] = dot(block[:, width : 2 * width], wout[...], NT).astype(BF)
            tracks[rows, :] = block[:, 2 * width :]
    for o in range(groups):
        if o:
            first[o].wait_send()
        to_y[o].wait_send()
        to_c[o].wait_send()
        to_d[o].wait_send()


def gather(pay, wqkv, wout, groups, width):
    cap, columns = pay.shape[1:]
    slots = groups * cap * 4
    sems = pltpu.SemaphoreType.DMA
    return pl.pallas_call(
        functools.partial(gather_kernel, groups, width),
        out_shape=(
            jax.ShapeDtypeStruct((slots, wqkv.shape[1]), BF),
            jax.ShapeDtypeStruct((slots, wout.shape[0]), BF),
            jax.ShapeDtypeStruct((slots, LANES), BF),
        ),
        in_specs=[VMEM] * 3,
        out_specs=(VMEM,) * 3,
        scratch_shapes=[
            pltpu.VMEM((groups, 4, cap, columns), BF),
            sems((groups,)), sems((groups,)), sems((groups,)), sems((groups,)),
            sems((groups, 2)), sems((groups, 2)),
        ],
        compiler_params=pltpu.CompilerParams(
            collective_id=0, has_side_effects=True, vmem_limit_bytes=48 * 2**20
        ),
    )(pay, wqkv, wout)


def scatter_kernel(groups, width, att, dqkv, wqkv, wout, out, part, near, total, passed, crossed, ready, s_dp, r_dp, s_y, r_y, s_c, r_c):
    far, sibling, across, me = partners_of(groups)
    greet(far[1:] + [sibling, across])
    cap = out.shape[1]

    def remote(src, dst, send, recv, device):
        return pltpu.make_async_remote_copy(
            src_ref=src, dst_ref=dst, send_sem=send, recv_sem=recv, device_id=device, device_id_type=MESH
        )

    to_c = [
        [remote(part.at[o, 2 * j + 1], near.at[o, j], s_c.at[o, j], r_c.at[o, j], sibling) for j in (0, 1)]
        for o in range(groups)
    ]
    to_y = [remote(passed.at[o], crossed.at[o], s_y.at[o], r_y.at[o], across) for o in range(groups)]
    home = [
        remote(ready.at[o], out.at[o], s_dp.at[o], r_dp.at[o], far[o]) if o else None
        for o in range(groups)
    ]
    half = groups // 2
    order = list(range(half, groups)) + list(range(1, half)) + [0]

    def compute(o):
        rows = pl.ds(o * 4 * cap, 4 * cap)
        part[o, :, :, :width] = dot(att[rows, :], wout[...]).astype(BF).reshape(4, cap, width)
        part[o, :, :, width:] = dot(dqkv[rows, :], wqkv[...], NT).astype(BF).reshape(4, cap, width)
        to_c[o][0].start()
        to_c[o][1].start()

    def middle(o):
        to_c[o][0].wait_recv()
        to_c[o][1].wait_recv()
        passed[o] = (part[o, 2].astype(F32) + near[o, 1].astype(F32)).astype(BF)
        to_y[o].start()
        total[o] = (part[o, 0].astype(F32) + near[o, 0].astype(F32)).astype(BF)

    def last(o):
        to_y[o].wait_recv()
        value = (total[o].astype(F32) + crossed[o].astype(F32)).astype(BF)
        if o:
            ready[o] = value
            home[o].start()
        else:
            out[0] = value

    for step in range(groups + 2):
        if step < groups:
            compute(order[step])
        if 1 <= step <= groups:
            middle(order[step - 1])
        if step >= 2:
            last(order[step - 2])
    for o in order:
        to_c[o][0].wait_send()
        to_c[o][1].wait_send()
        to_y[o].wait_send()
        if o:
            home[o].wait()


def scatter(att, dqkv, wqkv, wout, groups, width):
    slots = att.shape[0]
    cap = slots // (4 * groups)
    sems = pltpu.SemaphoreType.DMA
    one = pltpu.VMEM((groups, cap, 2 * width), BF)
    return pl.pallas_call(
        functools.partial(scatter_kernel, groups, width),
        out_shape=jax.ShapeDtypeStruct((groups, cap, 2 * width), BF),
        in_specs=[VMEM] * 4,
        out_specs=VMEM,
        scratch_shapes=[
            pltpu.VMEM((groups, 4, cap, 2 * width), BF),
            pltpu.VMEM((groups, 2, cap, 2 * width), BF),
            one, one, one, one,
            sems((groups,)), sems((groups,)), sems((groups,)), sems((groups,)),
            sems((groups, 2)), sems((groups, 2)),
        ],
        compiler_params=pltpu.CompilerParams(
            collective_id=1, has_side_effects=True, vmem_limit_bytes=56 * 2**20
        ),
    )(att, dqkv, wqkv, wout)


def attention_kernel(tiles, query, key, value, grad, tq, tk, att, dq, dk, dv, dk_t, dv_t):
    tile = pl.program_id(1)
    q, k, v, g = query[...], key[...], value[...], grad[...]
    scores = jnp.where(tq[...] == tk[...], dot(q, k, NT) * SCALE, -1e30)
    top = jnp.max(scores, axis=1, keepdims=True)
    expo = jnp.exp(scores - top)
    prob = expo * (1.0 / jnp.sum(expo, axis=1, keepdims=True))
    weights = prob.astype(BF)
    result = dot(weights, v).astype(BF)
    att[...] = result
    delta = jnp.sum(g.astype(F32) * result.astype(F32), axis=1, keepdims=True)
    dscore = (prob * (dot(g, v, NT) - delta)).astype(BF)
    dq[...] = (dot(dscore, k) * SCALE).astype(BF)

    @pl.when(tile == 0)
    def _():
        dk_t[...] = jnp.zeros_like(dk_t)
        dv_t[...] = jnp.zeros_like(dv_t)

    dk_t[...] += dot(q, dscore, TN)
    dv_t[...] += dot(g, weights, TN)

    @pl.when(tile == tiles - 1)
    def _():
        dk[...] = (dk_t[...].T * SCALE).astype(BF)
        dv[...] = dv_t[...].T.astype(BF)


def attention(qkv, gatt, track):
    slots = qkv.shape[0]
    heads = gatt.shape[1] // LANES
    rows = min(256, slots)
    tiles = slots // rows
    whole = lambda first: pl.BlockSpec((slots, LANES), lambda h, t: (0, first + h))
    part = pl.BlockSpec((rows, LANES), lambda h, t: (t, h))
    out = jax.ShapeDtypeStruct((slots, heads * LANES), BF)
    return pl.pallas_call(
        functools.partial(attention_kernel, tiles),
        grid=(heads, tiles),
        out_shape=(out,) * 4,
        in_specs=[
            part, whole(heads), whole(2 * heads), part,
            pl.BlockSpec((rows, 1), lambda h, t: (t, 0)),
            pl.BlockSpec((1, slots), lambda h, t: (0, 0)),
        ],
        out_specs=(part, part, whole(0), whole(0)),
        scratch_shapes=[pltpu.VMEM((LANES, slots), F32), pltpu.VMEM((LANES, slots), F32)],
        compiler_params=pltpu.CompilerParams(vmem_limit_bytes=48 * 2**20),
    )(qkv, qkv, qkv, gatt, track[:, None], track[None, :])


def normalize(rows, gain):
    mean = jnp.mean(rows, axis=1, keepdims=True)
    centred = rows - mean
    var = jnp.mean(centred * centred, axis=1, keepdims=True)
    return centred * lax.rsqrt(var + 1e-06) * gain[None, :]


def local(tokens, gain, w_qkv, w_out, dest, track, cotangent):
    count, width = tokens.shape
    groups, parts = lax.axis_size("dp"), lax.axis_size("seq")
    capacity = 2 * count // groups
    slots = groups * capacity
    heads = HEADS // parts
    me, part = lax.axis_index("dp"), lax.axis_index("seq")
    own = capacity % 16 == 0 and parts == 4

    clip_group = dest[:, 0]
    onehot = (clip_group[:, None] == jnp.arange(groups, dtype=jnp.int32)[None, :]).astype(jnp.int32)
    rank = jnp.sum(jnp.cumsum(onehot, axis=0) * onehot, axis=1) - 1
    slot_ids = jnp.arange(slots, dtype=jnp.int32)
    placing = (clip_group * capacity + rank)[None, :] == slot_ids[:, None]
    group_back = clip_group ^ me if own else clip_group
    placing_back = (group_back * capacity + rank)[:, None] == slot_ids[None, :]

    rows_f = tokens.astype(F32)
    normed, ln_back = jax.vjp(lambda value: normalize(value, gain), rows_f)
    marks = jnp.broadcast_to((track + 1).astype(BF)[:, None], (count, LANES))
    payload = jnp.concatenate([normed.astype(BF), cotangent, marks], axis=1)
    payload = dot(placing.astype(BF), payload).astype(BF).reshape(groups, capacity, -1)

    pad = LANES - HEAD
    mine = lax.dynamic_index_in_dim(w_qkv.reshape(width, 3, parts, heads, HEAD), part, 2, keepdims=False)
    mine = jnp.pad(mine, ((0, 0), (0, 0), (0, 0), (0, pad))).reshape(width, 3 * heads * LANES)
    mine_out = lax.dynamic_index_in_dim(w_out.reshape(parts, heads, HEAD, width), part, 0, keepdims=False)
    mine_out = jnp.pad(mine_out, ((0, 0), (0, pad), (0, 0))).reshape(heads * LANES, width)

    if own:
        qkv, gatt, marked = gather(payload, mine, mine_out, groups, width)
    else:
        moved = lax.all_to_all(payload.reshape(slots, -1), "dp", split_axis=0, concat_axis=0, tiled=True)
        moved = lax.all_gather(moved, "seq", axis=0, tiled=True)
        qkv = dot(moved[:, :width], mine).astype(BF)
        gatt = dot(moved[:, width : 2 * width], mine_out, NT).astype(BF)
        marked = moved[:, 2 * width :]

    att, dq, dk, dv = attention(qkv, gatt, marked[:, 0].astype(F32))
    dqkv = jnp.concatenate([dq, dk, dv], axis=1)

    if own:
        back = scatter(att, dqkv, mine, mine_out, groups, width)
    else:
        sums = jnp.concatenate([dot(att, mine_out), dot(dqkv, mine, NT)], axis=1).astype(BF)
        sums = lax.all_to_all(sums.reshape(parts, slots, -1), "seq", split_axis=0, concat_axis=0, tiled=True)
        sums = jnp.sum(sums.astype(F32), axis=0).astype(BF)
        back = lax.all_to_all(sums, "dp", split_axis=0, concat_axis=0, tiled=True)

    back = dot(placing_back.astype(BF), back.reshape(slots, 2 * width))
    output = (rows_f + back[:, :width]).astype(BF)
    grad_tokens = (cotangent.astype(F32) + ln_back(back[:, width:])[0]).astype(BF)
    return (output, grad_tokens)


def solution(mesh):
    return jax.shard_map(
        local,
        mesh=mesh,
        in_specs=(
            P(("dp", "seq"), None),
            P(),
            P(),
            P(),
            P(("dp", "seq"), None),
            P(("dp", "seq")),
            P(("dp", "seq"), None),
        ),
        out_specs=(P(("dp", "seq"), None), P(("dp", "seq"), None)),
        check_vma=False,
    )
```

```python
import functools

import jax
import jax.numpy as jnp
from jax import lax
from jax.experimental import pallas as pl
from jax.experimental.pallas import tpu as pltpu
from jax.sharding import PartitionSpec as P

HEADS = 16
HEAD = 72
LANES = 128
WINDOW = 3
SCALE = HEAD ** (-0.5)
MESH = pl.DeviceIdType.MESH
VMEM = pl.BlockSpec(memory_space=pltpu.VMEM)
BF = jnp.bfloat16
F32 = jnp.float32
NT = (((1,), (1,)), ((), ()))
TN = (((0,), (0,)), ((), ()))


def dot(a, b, dims=(((1,), (0,)), ((), ()))):
    return lax.dot_general(a, b, dims, preferred_element_type=F32)


def flip(index, mask):
    bit = 1
    out = index
    while bit <= mask:
        if mask & bit:
            out = out + bit * (1 - 2 * ((index // bit) % 2))
        bit *= 2
    return out


def greet(partners):
    barrier = pltpu.get_barrier_semaphore()
    for device in partners:
        pl.semaphore_signal(barrier, inc=1, device_id=device, device_id_type=MESH)
    pl.semaphore_wait(barrier, len(partners))


def partners_of(groups):
    me, part = lax.axis_index("dp"), lax.axis_index("seq")
    far = [(flip(me, o), part) for o in range(groups)]
    return far, (me, flip(part, 1)), (me, flip(part, 2)), me


def select_heads(width, heads, whole, whole_out, wqkv, wout):
    first = lax.axis_index("seq") * (heads * HEAD)
    span = heads * LANES
    row = lax.broadcasted_iota(jnp.int32, (width, span), 0)
    column = lax.broadcasted_iota(jnp.int32, (width, span), 1)
    pick = jnp.zeros((width, span), jnp.bool_)
    for j in range(heads):
        inside = (column >= j * LANES) & (column < j * LANES + HEAD)
        pick = pick | (inside & (row == column + (first + j * (HEAD - LANES))))
    pick = pick.astype(F32).astype(BF)

    def some_rows(i, carry):
        rows = pl.ds(pl.multiple_of(i * LANES, LANES), LANES)
        for j in range(3):
            wqkv[rows, j * span : (j + 1) * span] = dot(whole[rows, j * width : (j + 1) * width], pick).astype(BF)
        return carry

    lax.fori_loop(0, width // LANES, some_rows, 0)
    for j in range(heads):
        row = lax.broadcasted_iota(jnp.int32, (LANES, width), 0)
        column = lax.broadcasted_iota(jnp.int32, (LANES, width), 1)
        pick = ((row < HEAD) & (column == row + (first + j * HEAD))).astype(F32).astype(BF)
        wout[j * LANES : (j + 1) * LANES, :] = dot(pick, whole_out[...]).astype(BF)


def gather_kernel(groups, width, heads, pay, w_qkv, w_out, qkv, gatt, tracks, wqkv, wout, held, whole, whole_out, s_w, s_dp, r_dp, s_y, r_y, s_c, r_c):
    far, sibling, across, me = partners_of(groups)
    load = pltpu.make_async_copy(w_qkv, whole, s_w.at[0])
    load_out = pltpu.make_async_copy(w_out, whole_out, s_w.at[1])
    load.start()
    load_out.start()
    greet(far[1:] + [sibling, across])
    cap = pay.shape[1]

    def remote(src, dst, send, recv, device):
        return pltpu.make_async_remote_copy(
            src_ref=src, dst_ref=dst, send_sem=send, recv_sem=recv, device_id=device, device_id_type=MESH
        )

    first = [
        remote(pay.at[far[o][0]], held.at[o, 0], s_dp.at[o], r_dp.at[o], far[o]) if o else None
        for o in range(groups)
    ]
    half = groups // 2
    queue = [half]
    for o in range(1, half):
        queue += [o, half + o]
    order = [0] + queue
    for o in queue[:WINDOW]:
        first[o].start()
    held[0, 0] = pay[me]
    to_y = [remote(held.at[o, 0], held.at[o, 2], s_y.at[o], r_y.at[o], across) for o in range(groups)]
    to_c = [remote(held.at[o, 0], held.at[o, 1], s_c.at[o, 0], r_c.at[o, 0], sibling) for o in range(groups)]
    to_d = [remote(held.at[o, 2], held.at[o, 3], s_c.at[o, 1], r_c.at[o, 1], sibling) for o in range(groups)]
    def arrive(step):
        o = order[step]
        if step:
            first[o].wait()
            if step + WINDOW <= len(queue):
                first[queue[step + WINDOW - 1]].start()
        to_y[o].start()
        to_c[o].start()

    def forward(step):
        o = order[step]
        to_y[o].wait_recv()
        to_d[o].start()

    def project(step):
        o = order[step]
        to_c[o].wait_recv()
        to_d[o].wait_recv()
        block = held[o].reshape(4 * cap, held.shape[3])
        rows = pl.ds(o * 4 * cap, 4 * cap)
        qkv[rows, :] = dot(block[:, :width], wqkv[...]).astype(BF)
        gatt[rows, :] = dot(block[:, width : 2 * width], wout[...], NT).astype(BF)
        tracks[rows, :] = block[:, 2 * width :]

    for step in range(groups + 2):
        if step < groups:
            arrive(step)
        if step == 0:
            load.wait()
            load_out.wait()
            select_heads(width, heads, whole, whole_out, wqkv, wout)
        if 1 <= step <= groups:
            forward(step - 1)
        if step >= 2:
            project(step - 2)
    for o in range(groups):
        to_y[o].wait_send()
        to_c[o].wait_send()
        to_d[o].wait_send()


def gather(pay, w_qkv, w_out, groups, width, heads):
    cap, columns = pay.shape[1:]
    slots = groups * cap * 4
    span = heads * LANES
    sems = pltpu.SemaphoreType.DMA
    return pl.pallas_call(
        functools.partial(gather_kernel, groups, width, heads),
        out_shape=(
            jax.ShapeDtypeStruct((slots, 3 * span), BF),
            jax.ShapeDtypeStruct((slots, span), BF),
            jax.ShapeDtypeStruct((slots, LANES), BF),
            jax.ShapeDtypeStruct((width, 3 * span), BF),
            jax.ShapeDtypeStruct((span, width), BF),
        ),
        in_specs=[VMEM, pl.BlockSpec(memory_space=pl.ANY), pl.BlockSpec(memory_space=pl.ANY)],
        out_specs=(VMEM,) * 5,
        scratch_shapes=[
            pltpu.VMEM((groups, 4, cap, columns), BF),
            pltpu.VMEM(w_qkv.shape, BF),
            pltpu.VMEM(w_out.shape, BF),
            sems((2,)),
            sems((groups,)), sems((groups,)), sems((groups,)), sems((groups,)),
            sems((groups, 2)), sems((groups, 2)),
        ],
        compiler_params=pltpu.CompilerParams(
            collective_id=0, has_side_effects=True, vmem_limit_bytes=56 * 2**20
        ),
    )(pay, w_qkv, w_out)


def scatter_kernel(groups, width, att, dq, dk, dv, wqkv, wout, out, part, near, total, passed, crossed, ready, s_dp, r_dp, s_y, r_y, s_c, r_c):
    far, sibling, across, me = partners_of(groups)
    greet(far[1:] + [sibling, across])
    cap = out.shape[1]

    def remote(src, dst, send, recv, device):
        return pltpu.make_async_remote_copy(
            src_ref=src, dst_ref=dst, send_sem=send, recv_sem=recv, device_id=device, device_id_type=MESH
        )

    to_c = [
        [remote(part.at[o, 2 * j + 1], near.at[o, j], s_c.at[o, j], r_c.at[o, j], sibling) for j in (0, 1)]
        for o in range(groups)
    ]
    to_y = [remote(passed.at[o], crossed.at[o], s_y.at[o], r_y.at[o], across) for o in range(groups)]
    home = [
        remote(ready.at[o], out.at[o], s_dp.at[o], r_dp.at[o], far[o]) if o else None
        for o in range(groups)
    ]
    half = groups // 2
    order = list(range(half, groups)) + list(range(1, half)) + [0]

    def compute(o):
        rows = pl.ds(o * 4 * cap, 4 * cap)
        part[o, :, :, :width] = dot(att[rows, :], wout[...]).astype(BF).reshape(4, cap, width)
        span = att.shape[1]
        normed = dot(dq[rows, :], wqkv[:, :span], NT)
        normed += dot(dk[rows, :], wqkv[:, span : 2 * span], NT)
        normed += dot(dv[rows, :], wqkv[:, 2 * span :], NT)
        part[o, :, :, width:] = normed.astype(BF).reshape(4, cap, width)
        to_c[o][0].start()
        to_c[o][1].start()

    def middle(o):
        to_c[o][0].wait_recv()
        to_c[o][1].wait_recv()
        passed[o] = (part[o, 2].astype(F32) + near[o, 1].astype(F32)).astype(BF)
        to_y[o].start()
        total[o] = (part[o, 0].astype(F32) + near[o, 0].astype(F32)).astype(BF)

    def last(o):
        to_y[o].wait_recv()
        value = (total[o].astype(F32) + crossed[o].astype(F32)).astype(BF)
        if o:
            ready[o] = value
            home[o].start()
        else:
            out[0] = value

    for step in range(groups + 2):
        if step < groups:
            compute(order[step])
        if 1 <= step <= groups:
            middle(order[step - 1])
        if step >= 2:
            last(order[step - 2])
    for o in order:
        to_c[o][0].wait_send()
        to_c[o][1].wait_send()
        to_y[o].wait_send()
        if o:
            home[o].wait()


def scatter(att, dq, dk, dv, wqkv, wout, groups, width):
    slots = att.shape[0]
    cap = slots // (4 * groups)
    sems = pltpu.SemaphoreType.DMA
    one = pltpu.VMEM((groups, cap, 2 * width), BF)
    return pl.pallas_call(
        functools.partial(scatter_kernel, groups, width),
        out_shape=jax.ShapeDtypeStruct((groups, cap, 2 * width), BF),
        in_specs=[VMEM] * 6,
        out_specs=VMEM,
        scratch_shapes=[
            pltpu.VMEM((groups, 4, cap, 2 * width), BF),
            pltpu.VMEM((groups, 2, cap, 2 * width), BF),
            one, one, one, one,
            sems((groups,)), sems((groups,)), sems((groups,)), sems((groups,)),
            sems((groups, 2)), sems((groups, 2)),
        ],
        compiler_params=pltpu.CompilerParams(
            collective_id=1, has_side_effects=True, vmem_limit_bytes=56 * 2**20
        ),
    )(att, dq, dk, dv, wqkv, wout)


def attention_kernel(tiles, query, key, value, grad, tq, tk, att, dq, dk, dv, dk_t, dv_t):
    tile = pl.program_id(1)
    q, k, v, g = query[...], key[...], value[...], grad[...]
    scores = jnp.where(tq[...] == tk[...], dot(q, k, NT) * SCALE, -1e30)
    top = jnp.max(scores, axis=1, keepdims=True)
    expo = jnp.exp(scores - top)
    prob = expo * (1.0 / jnp.sum(expo, axis=1, keepdims=True))
    weights = prob.astype(BF)
    result = dot(weights, v).astype(BF)
    att[...] = result
    delta = jnp.sum(g.astype(F32) * result.astype(F32), axis=1, keepdims=True)
    dscore = (prob * (dot(g, v, NT) - delta)).astype(BF)
    dq[...] = (dot(dscore, k) * SCALE).astype(BF)

    @pl.when(tile == 0)
    def _():
        dk_t[...] = jnp.zeros_like(dk_t)
        dv_t[...] = jnp.zeros_like(dv_t)

    dk_t[...] += dot(q, dscore, TN)
    dv_t[...] += dot(g, weights, TN)

    @pl.when(tile == tiles - 1)
    def _():
        dk[...] = (dk_t[...].T * SCALE).astype(BF)
        dv[...] = dv_t[...].T.astype(BF)


def attention(qkv, gatt, track):
    slots = qkv.shape[0]
    heads = gatt.shape[1] // LANES
    rows = min(256, slots)
    tiles = slots // rows
    whole = lambda first: pl.BlockSpec((slots, LANES), lambda h, t: (0, first + h))
    part = pl.BlockSpec((rows, LANES), lambda h, t: (t, h))
    out = jax.ShapeDtypeStruct((slots, heads * LANES), BF)
    return pl.pallas_call(
        functools.partial(attention_kernel, tiles),
        grid=(heads, tiles),
        out_shape=(out,) * 4,
        in_specs=[
            part, whole(heads), whole(2 * heads), part,
            pl.BlockSpec((rows, 1), lambda h, t: (t, 0)),
            pl.BlockSpec((1, slots), lambda h, t: (0, 0)),
        ],
        out_specs=(part, part, whole(0), whole(0)),
        scratch_shapes=[pltpu.VMEM((LANES, slots), F32), pltpu.VMEM((LANES, slots), F32)],
        compiler_params=pltpu.CompilerParams(vmem_limit_bytes=48 * 2**20),
    )(qkv, qkv, qkv, gatt, track[:, None], track[None, :])


def normalize(rows, gain):
    mean = jnp.mean(rows, axis=1, keepdims=True)
    centred = rows - mean
    var = jnp.mean(centred * centred, axis=1, keepdims=True)
    return centred * lax.rsqrt(var + 1e-06) * gain[None, :]


def local(tokens, gain, w_qkv, w_out, dest, track, cotangent):
    count, width = tokens.shape
    groups, parts = lax.axis_size("dp"), lax.axis_size("seq")
    capacity = 2 * count // groups
    slots = groups * capacity
    heads = HEADS // parts
    me, part = lax.axis_index("dp"), lax.axis_index("seq")
    own = capacity % 16 == 0 and parts == 4

    clip_group = dest[:, 0]
    onehot = (clip_group[:, None] == jnp.arange(groups, dtype=jnp.int32)[None, :]).astype(jnp.int32)
    rank = jnp.sum(jnp.cumsum(onehot, axis=0) * onehot, axis=1) - 1
    slot_ids = jnp.arange(slots, dtype=jnp.int32)
    placing = (clip_group * capacity + rank)[None, :] == slot_ids[:, None]
    group_back = clip_group ^ me if own else clip_group
    placing_back = (group_back * capacity + rank)[:, None] == slot_ids[None, :]

    rows_f = tokens.astype(F32)
    normed, ln_back = jax.vjp(lambda value: normalize(value, gain), rows_f)
    marks = jnp.broadcast_to((track + 1).astype(BF)[:, None], (count, LANES))
    payload = jnp.concatenate([normed.astype(BF), cotangent, marks], axis=1)
    payload = dot(placing.astype(BF), payload).astype(BF).reshape(groups, capacity, -1)

    if own:
        qkv, gatt, marked, mine, mine_out = gather(payload, w_qkv, w_out, groups, width, heads)
    else:
        pad = LANES - HEAD
        mine = lax.dynamic_index_in_dim(w_qkv.reshape(width, 3, parts, heads, HEAD), part, 2, keepdims=False)
        mine = jnp.pad(mine, ((0, 0), (0, 0), (0, 0), (0, pad))).reshape(width, 3 * heads * LANES)
        mine_out = lax.dynamic_index_in_dim(w_out.reshape(parts, heads, HEAD, width), part, 0, keepdims=False)
        mine_out = jnp.pad(mine_out, ((0, 0), (0, pad), (0, 0))).reshape(heads * LANES, width)
        moved = lax.all_to_all(payload.reshape(slots, -1), "dp", split_axis=0, concat_axis=0, tiled=True)
        moved = lax.all_gather(moved, "seq", axis=0, tiled=True)
        qkv = dot(moved[:, :width], mine).astype(BF)
        gatt = dot(moved[:, width : 2 * width], mine_out, NT).astype(BF)
        marked = moved[:, 2 * width :]

    att, dq, dk, dv = attention(qkv, gatt, marked[:, 0].astype(F32))

    if own:
        back = scatter(att, dq, dk, dv, mine, mine_out, groups, width)
    else:
        dqkv = jnp.concatenate([dq, dk, dv], axis=1)
        sums = jnp.concatenate([dot(att, mine_out), dot(dqkv, mine, NT)], axis=1).astype(BF)
        sums = lax.all_to_all(sums.reshape(parts, slots, -1), "seq", split_axis=0, concat_axis=0, tiled=True)
        sums = jnp.sum(sums.astype(F32), axis=0).astype(BF)
        back = lax.all_to_all(sums, "dp", split_axis=0, concat_axis=0, tiled=True)

    back = dot(placing_back.astype(BF), back.reshape(slots, 2 * width))
    output = (rows_f + back[:, :width]).astype(BF)
    grad_tokens = (cotangent.astype(F32) + ln_back(back[:, width:])[0]).astype(BF)
    return (output, grad_tokens)


def solution(mesh):
    return jax.shard_map(
        local,
        mesh=mesh,
        in_specs=(
            P(("dp", "seq"), None),
            P(),
            P(),
            P(),
            P(("dp", "seq"), None),
            P(("dp", "seq")),
            P(("dp", "seq"), None),
        ),
        out_specs=(P(("dp", "seq"), None), P(("dp", "seq"), None)),
        check_vma=False,
    )
```

```python
import functools

import jax
import jax.numpy as jnp
from jax import lax
from jax.experimental import pallas as pl
from jax.experimental.pallas import tpu as pltpu
from jax.sharding import PartitionSpec as P

HEADS = 16
HEAD = 72
LANES = 128
SCALE = HEAD ** (-0.5)
MESH = pl.DeviceIdType.MESH
VMEM = pl.BlockSpec(memory_space=pltpu.VMEM)
BF = jnp.bfloat16
F32 = jnp.float32
NT = (((1,), (1,)), ((), ()))
TN = (((0,), (0,)), ((), ()))


def dot(a, b, dims=(((1,), (0,)), ((), ()))):
    return lax.dot_general(a, b, dims, preferred_element_type=F32)


def flip(index, mask):
    bit = 1
    out = index
    while bit <= mask:
        if mask & bit:
            out = out + bit * (1 - 2 * ((index // bit) % 2))
        bit *= 2
    return out


def partners_of(groups):
    me, part = lax.axis_index("dp"), lax.axis_index("seq")
    far = [(flip(me, o), part) for o in range(groups)]
    return far, (me, flip(part, 1)), (me, flip(part, 2)), me


def picks(width, heads, first):
    span = heads * LANES
    row = lax.broadcasted_iota(jnp.int32, (width, span), 0)
    column = lax.broadcasted_iota(jnp.int32, (width, span), 1)
    pick = jnp.zeros((width, span), jnp.bool_)
    for j in range(heads):
        inside = (column >= j * LANES) & (column < j * LANES + HEAD)
        pick = pick | (inside & (row == column + (first + j * (HEAD - LANES))))
    return pick.astype(F32).astype(BF)


def remote(src, dst, send, recv, device):
    return pltpu.make_async_remote_copy(
        src_ref=src, dst_ref=dst, send_sem=send, recv_sem=recv, device_id=device, device_id_type=MESH
    )


class Gather:
    def __init__(self, order, places, pay, held, sems):
        far, sibling, across, me = places
        s_dp, r_dp, s_y, r_y, s_c, r_c = sems
        self.order, self.pay, self.held, self.me = order, pay, held, me
        n = len(order)
        self.first = [
            remote(pay.at[far[o][0]], held.at[o, 0], s_dp.at[o], r_dp.at[o], far[o]) if o else None
            for o in range(n)
        ]
        self.to_y = [remote(held.at[o, 0], held.at[o, 2], s_y.at[o], r_y.at[o], across) for o in range(n)]
        self.to_c = [remote(held.at[o, 0], held.at[o, 1], s_c.at[o, 0], r_c.at[o, 0], sibling) for o in range(n)]
        self.to_d = [remote(held.at[o, 2], held.at[o, 3], s_c.at[o, 1], r_c.at[o, 1], sibling) for o in range(n)]

    def send(self, step):
        o = self.order[step]
        if o:
            self.first[o].start()
        else:
            self.held[0, 0] = self.pay[self.me]

    def arrive(self, step):
        o = self.order[step]
        if o:
            self.first[o].wait()
        self.to_y[o].start()
        self.to_c[o].start()

    def forward(self, step):
        o = self.order[step]
        self.to_y[o].wait_recv()
        self.to_d[o].start()

    def ready(self, step):
        o = self.order[step]
        self.to_c[o].wait_recv()
        self.to_d[o].wait_recv()
        return o

    def finish(self):
        for o in range(len(self.order)):
            self.to_y[o].wait_send()
            self.to_c[o].wait_send()
            self.to_d[o].wait_send()


class Scatter:
    def __init__(self, order, places, part, near, total, passed, crossed, home, sems):
        far, sibling, across, _ = places
        s_dp, r_dp, s_y, r_y, s_c, r_c = sems
        self.order, self.part, self.near, self.total = order, part, near, total
        self.passed, self.crossed, self.home = passed, crossed, home
        n = len(order)
        self.to_c = [
            [remote(part.at[o, 2 * j + 1], near.at[o, j], s_c.at[o, j], r_c.at[o, j], sibling) for j in (0, 1)]
            for o in range(n)
        ]
        self.to_y = [remote(passed.at[o], crossed.at[o], s_y.at[o], r_y.at[o], across) for o in range(n)]
        self.to_home = [
            remote(total.at[o], home.at[o], s_dp.at[o], r_dp.at[o], far[o]) if o else None for o in range(n)
        ]

    def put(self, step, value):
        o = self.order[step]
        self.part[o] = value.reshape(self.part.shape[1:])
        self.to_c[o][0].start()
        self.to_c[o][1].start()

    def middle(self, step):
        o = self.order[step]
        self.to_c[o][0].wait_recv()
        self.to_c[o][1].wait_recv()
        self.passed[o] = (self.part[o, 2].astype(F32) + self.near[o, 1].astype(F32)).astype(BF)
        self.to_y[o].start()

    def last(self, step):
        o = self.order[step]
        self.to_y[o].wait_recv()
        value = self.part[o, 0].astype(F32) + self.near[o, 0].astype(F32) + self.crossed[o].astype(F32)
        if o:
            self.total[o] = value.astype(BF)
            self.to_home[o].start()
        else:
            self.home[0] = value.astype(BF)

    def finish(self):
        for o in range(len(self.order)):
            self.to_c[o][0].wait_send()
            self.to_c[o][1].wait_send()
            self.to_y[o].wait_send()
            if o:
                self.to_home[o].wait()


def fused_kernel(groups, heads, tokens, cotangent, gain, dest, track, w_qkv, w_out, output, grad_tokens,
                 pay_a, pay_b, held_a, held_b, whole, whole_out, wqkv, wout, qkv, gatt, att, dqkv,
                 tcol, trow, prob_s, dk_t, dv_t, part_a, part_b, near_a, near_b, total_a, total_b,
                 passed_a, passed_b, crossed_a, crossed_b, home_a, home_b, s_w, *sems):
    count, width = tokens.shape
    cap = pay_a.shape[1]
    slots, rows_all, span = groups * cap, groups * cap * 4, heads * LANES
    block = 4 * cap
    places = partners_of(groups)
    far, sibling, across, me = places
    barrier = pltpu.get_barrier_semaphore()
    greeted = far[1:] + [sibling, across]
    for device in greeted:
        pl.semaphore_signal(barrier, inc=1, device_id=device, device_id_type=MESH)
    load = pltpu.make_async_copy(w_qkv, whole, s_w.at[0])
    load_out = pltpu.make_async_copy(w_out, whole_out, s_w.at[1])
    load.start()
    load_out.start()

    x = tokens[...].astype(F32)
    centred = x - jnp.mean(x, axis=1, keepdims=True)
    scale = lax.rsqrt(jnp.mean(centred * centred, axis=1, keepdims=True) + 1e-06)
    normed = (centred * scale * gain[...]).astype(BF)
    group = dest[...]
    lane = lax.broadcasted_iota(jnp.int32, (count, LANES), 1)
    onehot = (group == lane).astype(F32)
    row = lax.broadcasted_iota(jnp.int32, (count, count), 0)
    column = lax.broadcasted_iota(jnp.int32, (count, count), 1)
    before = dot((column < row).astype(F32).astype(BF), onehot.astype(BF))
    rank = jnp.sum(before * onehot, axis=1, keepdims=True).astype(jnp.int32)
    slot = lax.broadcasted_iota(jnp.int32, (count, slots), 1)
    placing = (group * cap + rank == slot).astype(F32).astype(BF)
    placing_back = ((group ^ me) * cap + rank == slot).astype(F32).astype(BF)
    marks = jnp.broadcast_to((track[...] + 1).astype(F32), (count, LANES)).astype(BF)
    pay_a[:, :, :width] = dot(placing, normed, TN).astype(BF).reshape(groups, cap, width)
    pay_a[:, :, width:] = dot(placing, marks, TN).astype(BF).reshape(groups, cap, LANES)
    pay_b[...] = dot(placing, cotangent[...], TN).astype(BF).reshape(groups, cap, width)
    pl.semaphore_wait(barrier, len(greeted))

    half = groups // 2
    order = [0]
    for i in range(half):
        order += [half + i] + ([i + 1] if i + 1 < half else [])
    a = Gather(order, places, pay_a, held_a, [s.at[0] for s in sems])
    b = Gather(order, places, pay_b, held_b, [s.at[1] for s in sems])
    for step in range(groups):
        a.send(step)

    mine = lax.axis_index("seq") * (heads * HEAD)

    def select(start, stop):
        pick = picks(width, heads, mine)

        def some_rows(i, carry):
            rows = pl.ds(pl.multiple_of(i * LANES, LANES), LANES)
            for j in range(3):
                wqkv[rows, j * span : (j + 1) * span] = dot(whole[rows, j * width : (j + 1) * width], pick).astype(BF)
            return carry

        lax.fori_loop(start, stop, some_rows, 0)

    def project(step):
        o = a.ready(step)
        rows = pl.ds(o * block, block)
        held = held_a[o].reshape(block, width + LANES)
        qkv[rows, :] = dot(held[:, :width], wqkv[...]).astype(BF)
        marked = held[:, width:]
        tcol[rows, :] = marked
        first = (lax.broadcasted_iota(jnp.int32, (8, LANES), 1) == 0).astype(F32).astype(BF)
        trow[:, o * block : (o + 1) * block] = dot(first, marked, NT)

    def project_grad(step):
        o = b.ready(step)
        held = held_b[o].reshape(block, width)
        gatt[o * block : (o + 1) * block, :] = dot(held, wout[...], NT).astype(BF)

    chunks = width // LANES
    for step in range(groups + 3):
        if step < groups:
            a.arrive(step)
            b.send(step)
        if step == 0:
            load.wait()
        if 1 <= step <= groups:
            a.forward(step - 1)
        if step < 3:
            select(chunks * step // 3, chunks * (step + 1) // 3)
        if step >= 3:
            project(step - 3)
    load_out.wait()
    for j in range(heads):
        row = lax.broadcasted_iota(jnp.int32, (LANES, width), 0)
        column = lax.broadcasted_iota(jnp.int32, (LANES, width), 1)
        pick = ((row < HEAD) & (column == row + (mine + j * HEAD))).astype(F32).astype(BF)
        wout[j * LANES : (j + 1) * LANES, :] = dot(pick, whole_out[...]).astype(BF)

    tile = 256

    def head(h, base=0):
        return slice(base * span + h * LANES, base * span + (h + 1) * LANES)

    def attend(h):
        def some(t, carry):
            rows = pl.ds(pl.multiple_of(t * tile, tile), tile)
            match = tcol[rows, 0:1].astype(F32) == trow[0:1, :]
            scores = jnp.where(match, dot(qkv[rows, head(h)], qkv[:, head(h, 1)], NT) * SCALE, -1e30)
            expo = jnp.exp(scores - jnp.max(scores, axis=1, keepdims=True))
            weights = (expo * (1.0 / jnp.sum(expo, axis=1, keepdims=True))).astype(BF)
            prob_s[h, rows, :] = weights
            att[rows, head(h)] = dot(weights, qkv[:, head(h, 2)]).astype(BF)
            return carry

        lax.fori_loop(0, rows_all // tile, some, 0)

    def attend_back(h):
        dk_t[...] = jnp.zeros_like(dk_t)
        dv_t[...] = jnp.zeros_like(dv_t)

        def some(t, carry):
            rows = pl.ds(pl.multiple_of(t * tile, tile), tile)
            weights = prob_s[h, rows, :]
            g = gatt[rows, head(h)]
            delta = jnp.sum(g.astype(F32) * att[rows, head(h)].astype(F32), axis=1, keepdims=True)
            dscore = (weights.astype(F32) * (dot(g, qkv[:, head(h, 2)], NT) - delta)).astype(BF)
            dqkv[rows, head(h)] = (dot(dscore, qkv[:, head(h, 1)]) * SCALE).astype(BF)
            dk_t[...] += dot(qkv[rows, head(h)], dscore, TN)
            dv_t[...] += dot(g, weights, TN)
            return carry

        lax.fori_loop(0, rows_all // tile, some, 0)
        dqkv[:, head(h, 1)] = (dk_t[...].T * SCALE).astype(BF)
        dqkv[:, head(h, 2)] = dv_t[...].T.astype(BF)

    each = groups // heads
    for h in range(heads):
        for step in range(each * h, each * (h + 1)):
            b.arrive(step)
        for step in range(each * (h - 1), each * h):
            if step >= 0:
                b.forward(step)
        attend(h)
    for step in range(each * (heads - 1), groups):
        b.forward(step)

    home_order = list(range(half, groups)) + list(range(1, half)) + [0]
    out_a = Scatter(home_order, places, part_a, near_a, total_a, passed_a, crossed_a, home_a, [s.at[2] for s in sems])
    out_b = Scatter(home_order, places, part_b, near_b, total_b, passed_b, crossed_b, home_b, [s.at[3] for s in sems])
    for step in range(groups):
        o = home_order[step]
        out_a.put(step, dot(att[o * block : (o + 1) * block, :], wout[...]).astype(BF))
        if step:
            out_a.middle(step - 1)
    out_a.middle(groups - 1)
    for step in range(groups):
        project_grad(step)

    done = 0
    for h in range(heads):
        attend_back(h)
        until = min(groups, (h + 1) * ((groups + 2) // 3))
        for step in range(done, until):
            out_a.last(step)
        done = until
    for step in range(groups + 2):
        if step < groups:
            o = home_order[step]
            out_b.put(step, dot(dqkv[o * block : (o + 1) * block, :], wqkv[...], NT).astype(BF))
        if 1 <= step <= groups:
            out_b.middle(step - 1)
        if step >= 2:
            out_b.last(step - 2)
    a.finish()
    b.finish()
    out_a.finish()
    back = dot(placing_back, home_a[...].reshape(slots, width))
    output[...] = (tokens[...].astype(F32) + back).astype(BF)
    out_b.finish()
    back = dot(placing_back, home_b[...].reshape(slots, width)) * gain[...]
    x = tokens[...].astype(F32)
    unit = (x - jnp.mean(x, axis=1, keepdims=True)) * scale
    back = back - jnp.mean(back, axis=1, keepdims=True) - unit * jnp.mean(back * unit, axis=1, keepdims=True)
    grad_tokens[...] = (cotangent[...].astype(F32) + scale * back).astype(BF)


def fused(tokens, gain, w_qkv, w_out, dest, track, cotangent, groups, heads):
    count, width = tokens.shape
    cap = 2 * count // groups
    rows, span = groups * cap * 4, heads * LANES
    sems = pltpu.SemaphoreType.DMA
    buf = lambda *shape: pltpu.VMEM(shape, BF)
    out = jax.ShapeDtypeStruct((count, width), BF)
    anywhere = pl.BlockSpec(memory_space=pl.ANY)
    return pl.pallas_call(
        functools.partial(fused_kernel, groups, heads),
        out_shape=(out, out),
        in_specs=[VMEM] * 5 + [anywhere] * 2,
        out_specs=(VMEM, VMEM),
        scratch_shapes=[
            buf(groups, cap, width + LANES), buf(groups, cap, width),
            buf(groups, 4, cap, width + LANES), buf(groups, 4, cap, width),
            buf(*w_qkv.shape), buf(*w_out.shape),
            buf(width, 3 * span), buf(span, width),
            buf(rows, 3 * span), buf(rows, span), buf(rows, span), buf(rows, 3 * span),
            buf(rows, LANES), pltpu.VMEM((8, rows), F32),
            buf(heads, rows, rows),
            pltpu.VMEM((LANES, rows), F32), pltpu.VMEM((LANES, rows), F32),
            buf(groups, 4, cap, width), buf(groups, 4, cap, width),
            buf(groups, 2, cap, width), buf(groups, 2, cap, width),
        ]
        + [buf(groups, cap, width)] * 8
        + [sems((2,))]
        + [sems((4, groups))] * 4
        + [sems((4, groups, 2))] * 2,
        compiler_params=pltpu.CompilerParams(
            collective_id=0, has_side_effects=True, vmem_limit_bytes=62 * 2**20
        ),
    )(tokens, cotangent, gain[None, :], dest, track[:, None], w_qkv, w_out)


def attention_kernel(tiles, query, key, value, grad, tq, tk, att, dq, dk, dv, dk_t, dv_t):
    tile = pl.program_id(1)
    q, k, v, g = query[...], key[...], value[...], grad[...]
    scores = jnp.where(tq[...] == tk[...], dot(q, k, NT) * SCALE, -1e30)
    top = jnp.max(scores, axis=1, keepdims=True)
    expo = jnp.exp(scores - top)
    prob = expo * (1.0 / jnp.sum(expo, axis=1, keepdims=True))
    weights = prob.astype(BF)
    result = dot(weights, v).astype(BF)
    att[...] = result
    delta = jnp.sum(g.astype(F32) * result.astype(F32), axis=1, keepdims=True)
    dscore = (prob * (dot(g, v, NT) - delta)).astype(BF)
    dq[...] = (dot(dscore, k) * SCALE).astype(BF)

    @pl.when(tile == 0)
    def _():
        dk_t[...] = jnp.zeros_like(dk_t)
        dv_t[...] = jnp.zeros_like(dv_t)

    dk_t[...] += dot(q, dscore, TN)
    dv_t[...] += dot(g, weights, TN)

    @pl.when(tile == tiles - 1)
    def _():
        dk[...] = (dk_t[...].T * SCALE).astype(BF)
        dv[...] = dv_t[...].T.astype(BF)


def attention(qkv, gatt, track):
    slots = qkv.shape[0]
    heads = gatt.shape[1] // LANES
    rows = min(256, slots)
    tiles = slots // rows
    whole = lambda first: pl.BlockSpec((slots, LANES), lambda h, t: (0, first + h))
    part = pl.BlockSpec((rows, LANES), lambda h, t: (t, h))
    out = jax.ShapeDtypeStruct((slots, heads * LANES), BF)
    return pl.pallas_call(
        functools.partial(attention_kernel, tiles),
        grid=(heads, tiles),
        out_shape=(out,) * 4,
        in_specs=[
            part, whole(heads), whole(2 * heads), part,
            pl.BlockSpec((rows, 1), lambda h, t: (t, 0)),
            pl.BlockSpec((1, slots), lambda h, t: (0, 0)),
        ],
        out_specs=(part, part, whole(0), whole(0)),
        scratch_shapes=[pltpu.VMEM((LANES, slots), F32), pltpu.VMEM((LANES, slots), F32)],
        compiler_params=pltpu.CompilerParams(vmem_limit_bytes=48 * 2**20),
    )(qkv, qkv, qkv, gatt, track[:, None], track[None, :])


def normalize(rows, gain):
    mean = jnp.mean(rows, axis=1, keepdims=True)
    centred = rows - mean
    var = jnp.mean(centred * centred, axis=1, keepdims=True)
    return centred * lax.rsqrt(var + 1e-06) * gain[None, :]


def local(tokens, gain, w_qkv, w_out, dest, track, cotangent):
    count, width = tokens.shape
    groups, parts = lax.axis_size("dp"), lax.axis_size("seq")
    capacity = 2 * count // groups
    slots = groups * capacity
    heads = HEADS // parts
    part = lax.axis_index("seq")
    if capacity % 16 == 0 and parts == 4 and groups <= LANES:
        return fused(tokens, gain, w_qkv, w_out, dest, track, cotangent, groups, heads)

    clip_group = dest[:, 0]
    onehot = (clip_group[:, None] == jnp.arange(groups, dtype=jnp.int32)[None, :]).astype(jnp.int32)
    rank = jnp.sum(jnp.cumsum(onehot, axis=0) * onehot, axis=1) - 1
    slot_ids = jnp.arange(slots, dtype=jnp.int32)
    placing = (clip_group * capacity + rank)[None, :] == slot_ids[:, None]
    placing_back = (clip_group * capacity + rank)[:, None] == slot_ids[None, :]

    rows_f = tokens.astype(F32)
    normed, ln_back = jax.vjp(lambda value: normalize(value, gain), rows_f)
    marks = jnp.broadcast_to((track + 1).astype(BF)[:, None], (count, LANES))
    payload = jnp.concatenate([normed.astype(BF), cotangent, marks], axis=1)
    payload = dot(placing.astype(BF), payload).astype(BF).reshape(groups, capacity, -1)

    pad = LANES - HEAD
    mine = lax.dynamic_index_in_dim(w_qkv.reshape(width, 3, parts, heads, HEAD), part, 2, keepdims=False)
    mine = jnp.pad(mine, ((0, 0), (0, 0), (0, 0), (0, pad))).reshape(width, 3 * heads * LANES)
    mine_out = lax.dynamic_index_in_dim(w_out.reshape(parts, heads, HEAD, width), part, 0, keepdims=False)
    mine_out = jnp.pad(mine_out, ((0, 0), (0, pad), (0, 0))).reshape(heads * LANES, width)
    moved = lax.all_to_all(payload.reshape(slots, -1), "dp", split_axis=0, concat_axis=0, tiled=True)
    moved = lax.all_gather(moved, "seq", axis=0, tiled=True)
    qkv = dot(moved[:, :width], mine).astype(BF)
    gatt = dot(moved[:, width : 2 * width], mine_out, NT).astype(BF)
    marked = moved[:, 2 * width :]

    att, dq, dk, dv = attention(qkv, gatt, marked[:, 0].astype(F32))

    dqkv = jnp.concatenate([dq, dk, dv], axis=1)
    sums = jnp.concatenate([dot(att, mine_out), dot(dqkv, mine, NT)], axis=1).astype(BF)
    sums = lax.all_to_all(sums.reshape(parts, slots, -1), "seq", split_axis=0, concat_axis=0, tiled=True)
    sums = jnp.sum(sums.astype(F32), axis=0).astype(BF)
    back = lax.all_to_all(sums, "dp", split_axis=0, concat_axis=0, tiled=True)

    back = dot(placing_back.astype(BF), back.reshape(slots, 2 * width))
    output = (rows_f + back[:, :width]).astype(BF)
    grad_tokens = (cotangent.astype(F32) + ln_back(back[:, width:])[0]).astype(BF)
    return (output, grad_tokens)


def solution(mesh):
    return jax.shard_map(
        local,
        mesh=mesh,
        in_specs=(
            P(("dp", "seq"), None),
            P(),
            P(),
            P(),
            P(("dp", "seq"), None),
            P(("dp", "seq")),
            P(("dp", "seq"), None),
        ),
        out_specs=(P(("dp", "seq"), None), P(("dp", "seq"), None)),
        check_vma=False,
    )
```

```python
import functools

import jax
import jax.numpy as jnp
from jax import lax
from jax.experimental import pallas as pl
from jax.experimental.pallas import tpu as pltpu
from jax.sharding import PartitionSpec as P

HEADS = 16
HEAD = 72
LANES = 128
SCALE = HEAD ** (-0.5)
MESH = pl.DeviceIdType.MESH
VMEM = pl.BlockSpec(memory_space=pltpu.VMEM)
BF = jnp.bfloat16
F32 = jnp.float32
NT = (((1,), (1,)), ((), ()))
TN = (((0,), (0,)), ((), ()))


def dot(a, b, dims=(((1,), (0,)), ((), ()))):
    return lax.dot_general(a, b, dims, preferred_element_type=F32)


def flip(index, mask):
    bit = 1
    out = index
    while bit <= mask:
        if mask & bit:
            out = out + bit * (1 - 2 * ((index // bit) % 2))
        bit *= 2
    return out


def partners_of(groups):
    me, part = lax.axis_index("dp"), lax.axis_index("seq")
    far = [(flip(me, o), part) for o in range(groups)]
    return far, (me, flip(part, 1)), (me, flip(part, 2)), me


def picks(width, heads, first):
    span = heads * LANES
    row = lax.broadcasted_iota(jnp.int32, (width, span), 0)
    column = lax.broadcasted_iota(jnp.int32, (width, span), 1)
    pick = jnp.zeros((width, span), jnp.bool_)
    for j in range(heads):
        inside = (column >= j * LANES) & (column < j * LANES + HEAD)
        pick = pick | (inside & (row == column + (first + j * (HEAD - LANES))))
    return pick.astype(F32).astype(BF)


def remote(src, dst, send, recv, device):
    return pltpu.make_async_remote_copy(
        src_ref=src, dst_ref=dst, send_sem=send, recv_sem=recv, device_id=device, device_id_type=MESH
    )


class Gather:
    def __init__(self, order, places, pay, held, sems):
        far, sibling, across, me = places
        s_dp, r_dp, s_y, r_y, s_c, r_c = sems
        self.order, self.pay, self.held, self.me = order, pay, held, me
        n = len(order)
        self.first = [
            remote(pay.at[far[o][0]], held.at[o, 0], s_dp.at[o], r_dp.at[o], far[o]) if o else None
            for o in range(n)
        ]
        self.to_y = [remote(held.at[o, 0], held.at[o, 2], s_y.at[o], r_y.at[o], across) for o in range(n)]
        self.to_c = [remote(held.at[o, 0], held.at[o, 1], s_c.at[o, 0], r_c.at[o, 0], sibling) for o in range(n)]
        self.to_d = [remote(held.at[o, 2], held.at[o, 3], s_c.at[o, 1], r_c.at[o, 1], sibling) for o in range(n)]

    def send(self, step):
        o = self.order[step]
        if o:
            self.first[o].start()
        else:
            self.held[0, 0] = self.pay[self.me]

    def arrive(self, step):
        o = self.order[step]
        if o:
            self.first[o].wait()
        self.to_y[o].start()
        self.to_c[o].start()

    def forward(self, step):
        o = self.order[step]
        self.to_y[o].wait_recv()
        self.to_d[o].start()

    def ready(self, step):
        o = self.order[step]
        self.to_c[o].wait_recv()
        self.to_d[o].wait_recv()
        return o

    def finish(self):
        for o in range(len(self.order)):
            self.to_y[o].wait_send()
            self.to_c[o].wait_send()
            self.to_d[o].wait_send()


class Scatter:
    def __init__(self, order, places, part, near, total, passed, crossed, home, sems):
        far, sibling, across, _ = places
        s_dp, r_dp, s_y, r_y, s_c, r_c = sems
        self.order, self.part, self.near, self.total = order, part, near, total
        self.passed, self.crossed, self.home = passed, crossed, home
        n = len(order)
        self.to_c = [
            [remote(part.at[o, 2 * j + 1], near.at[o, j], s_c.at[o, j], r_c.at[o, j], sibling) for j in (0, 1)]
            for o in range(n)
        ]
        self.to_y = [remote(passed.at[o], crossed.at[o], s_y.at[o], r_y.at[o], across) for o in range(n)]
        self.to_home = [
            remote(total.at[o], home.at[o], s_dp.at[o], r_dp.at[o], far[o]) if o else None for o in range(n)
        ]

    def put(self, step, value):
        o = self.order[step]
        self.part[o] = value.reshape(self.part.shape[1:])
        self.to_c[o][0].start()
        self.to_c[o][1].start()

    def middle(self, step):
        o = self.order[step]
        self.to_c[o][0].wait_recv()
        self.to_c[o][1].wait_recv()
        self.passed[o] = (self.part[o, 2].astype(F32) + self.near[o, 1].astype(F32)).astype(BF)
        self.to_y[o].start()

    def last(self, step):
        o = self.order[step]
        self.to_y[o].wait_recv()
        value = self.part[o, 0].astype(F32) + self.near[o, 0].astype(F32) + self.crossed[o].astype(F32)
        if o:
            self.total[o] = value.astype(BF)
            self.to_home[o].start()
        else:
            self.home[0] = value.astype(BF)

    def finish(self):
        for o in range(len(self.order)):
            self.to_c[o][0].wait_send()
            self.to_c[o][1].wait_send()
            self.to_y[o].wait_send()
            if o:
                self.to_home[o].wait()


def fused_kernel(groups, heads, tokens, cotangent, gain, dest, track, w_qkv, w_out, output, grad_tokens,
                 pay_a, pay_b, held_a, held_b, whole, whole_out, wqkv, wout, qkv, gatt, att, dqkv,
                 tcol, trow, prob_s, dk_t, dv_t, part_a, part_b, near_a, near_b, total_a, total_b,
                 passed_a, passed_b, crossed_a, crossed_b, home_a, home_b, s_w, *sems):
    count, width = tokens.shape
    cap = pay_a.shape[1]
    slots, rows_all, span = groups * cap, groups * cap * 4, heads * LANES
    block = 4 * cap
    places = partners_of(groups)
    far, sibling, across, me = places
    barrier = pltpu.get_barrier_semaphore()
    greeted = far[1:] + [sibling, across]
    for device in greeted:
        pl.semaphore_signal(barrier, inc=1, device_id=device, device_id_type=MESH)
    load = pltpu.make_async_copy(w_qkv, whole, s_w.at[0])
    load_out = pltpu.make_async_copy(w_out, whole_out, s_w.at[1])
    load.start()
    load_out.start()

    x = tokens[...].astype(F32)
    centred = x - jnp.mean(x, axis=1, keepdims=True)
    scale = lax.rsqrt(jnp.mean(centred * centred, axis=1, keepdims=True) + 1e-06)
    normed = (centred * scale * gain[...]).astype(BF)
    row = lax.broadcasted_iota(jnp.int32, (count, count), 0)
    column = lax.broadcasted_iota(jnp.int32, (count, count), 1)
    upright = lambda line: jnp.sum(jnp.where(row == column, line, 0), axis=1, keepdims=True)
    group = upright(dest[...])
    lane = lax.broadcasted_iota(jnp.int32, (count, LANES), 1)
    onehot = (group == lane).astype(F32)
    before = dot((column < row).astype(F32).astype(BF), onehot.astype(BF))
    rank = jnp.sum(before * onehot, axis=1, keepdims=True).astype(jnp.int32)
    slot = lax.broadcasted_iota(jnp.int32, (count, slots), 1)
    placing = (group * cap + rank == slot).astype(F32).astype(BF)
    placing_back = ((group ^ me) * cap + rank == slot).astype(F32).astype(BF)
    marks = jnp.broadcast_to((upright(track[...]) + 1).astype(F32), (count, LANES)).astype(BF)
    pay_a[:, :, :width] = dot(placing, normed, TN).astype(BF).reshape(groups, cap, width)
    pay_a[:, :, width:] = dot(placing, marks, TN).astype(BF).reshape(groups, cap, LANES)
    pay_b[...] = dot(placing, cotangent[...], TN).astype(BF).reshape(groups, cap, width)
    pl.semaphore_wait(barrier, len(greeted))

    half = groups // 2
    order = []
    for i in range(0, half, 2):
        order += [i, i + 1, half + i, half + i + 1]
    a = Gather(order, places, pay_a, held_a, [s.at[0] for s in sems])
    b = Gather(order, places, pay_b, held_b, [s.at[1] for s in sems])
    for step in range(groups):
        a.send(step)

    mine = lax.axis_index("seq") * (heads * HEAD)

    def select(start, stop):
        pick = picks(width, heads, mine)

        def some_rows(i, carry):
            rows = pl.ds(pl.multiple_of(i * LANES, LANES), LANES)
            for j in range(3):
                wqkv[rows, j * span : (j + 1) * span] = dot(whole[rows, j * width : (j + 1) * width], pick).astype(BF)
            return carry

        lax.fori_loop(start, stop, some_rows, 0)

    def project(step):
        o = a.ready(step)
        a.ready(step + 1)
        rows = slice(o * block, (o + 2) * block)
        held = held_a[o : o + 2].reshape(2 * block, width + LANES)
        qkv[rows, :] = dot(held[:, :width], wqkv[...]).astype(BF)
        marked = held[:, width:]
        tcol[rows, :] = marked
        first = (lax.broadcasted_iota(jnp.int32, (8, LANES), 1) == 0).astype(F32).astype(BF)
        trow[:, rows] = dot(first, marked, NT)

    def project_grad(step):
        o = b.ready(step)
        b.ready(step + 1)
        held = held_b[o : o + 2].reshape(2 * block, width)
        gatt[o * block : (o + 2) * block, :] = dot(held, wout[...], NT).astype(BF)

    chunks = width // LANES
    for step in range(groups + 3):
        if step < groups:
            a.arrive(step)
            b.send(step)
        if step == 0:
            load.wait()
        if 1 <= step <= groups:
            a.forward(step - 1)
        if step < 3:
            select(chunks * step // 3, chunks * (step + 1) // 3)
        if step >= 3 and step % 2 == 0:
            project(step - 4)
    load_out.wait()
    for j in range(heads):
        row = lax.broadcasted_iota(jnp.int32, (LANES, width), 0)
        column = lax.broadcasted_iota(jnp.int32, (LANES, width), 1)
        pick = ((row < HEAD) & (column == row + (mine + j * HEAD))).astype(F32).astype(BF)
        wout[j * LANES : (j + 1) * LANES, :] = dot(pick, whole_out[...]).astype(BF)

    tile = 256

    def head(h, base=0):
        return slice(base * span + h * LANES, base * span + (h + 1) * LANES)

    def attend(h):
        def some(t, carry):
            rows = pl.ds(pl.multiple_of(t * tile, tile), tile)
            match = tcol[rows, 0:1].astype(F32) == trow[0:1, :]
            scores = jnp.where(match, dot(qkv[rows, head(h)], qkv[:, head(h, 1)], NT) * SCALE, -1e30)
            expo = jnp.exp(scores - jnp.max(scores, axis=1, keepdims=True))
            weights = (expo * (1.0 / jnp.sum(expo, axis=1, keepdims=True))).astype(BF)
            prob_s[h, rows, :] = weights
            att[rows, head(h)] = dot(weights, qkv[:, head(h, 2)]).astype(BF)
            return carry

        lax.fori_loop(0, rows_all // tile, some, 0)

    def attend_back(h):
        dk_t[...] = jnp.zeros_like(dk_t)
        dv_t[...] = jnp.zeros_like(dv_t)

        def some(t, carry):
            rows = pl.ds(pl.multiple_of(t * tile, tile), tile)
            weights = prob_s[h, rows, :]
            g = gatt[rows, head(h)]
            delta = jnp.sum(g.astype(F32) * att[rows, head(h)].astype(F32), axis=1, keepdims=True)
            dscore = (weights.astype(F32) * (dot(g, qkv[:, head(h, 2)], NT) - delta)).astype(BF)
            dqkv[rows, head(h)] = (dot(dscore, qkv[:, head(h, 1)]) * SCALE).astype(BF)
            dk_t[...] += dot(qkv[rows, head(h)], dscore, TN)
            dv_t[...] += dot(g, weights, TN)
            return carry

        lax.fori_loop(0, rows_all // tile, some, 0)
        dqkv[:, head(h, 1)] = (dk_t[...].T * SCALE).astype(BF)
        dqkv[:, head(h, 2)] = dv_t[...].T.astype(BF)

    each = groups // heads
    for h in range(heads):
        for step in range(each * h, each * (h + 1)):
            b.arrive(step)
        for step in range(each * (h - 1), each * h):
            if step >= 0:
                b.forward(step)
        attend(h)
    for step in range(each * (heads - 1), groups):
        b.forward(step)

    home_order = list(range(half, groups))
    for i in range(half - 2, 0, -2):
        home_order += [i, i + 1]
    home_order += [1, 0]
    out_a = Scatter(home_order, places, part_a, near_a, total_a, passed_a, crossed_a, home_a, [s.at[2] for s in sems])
    out_b = Scatter(home_order, places, part_b, near_b, total_b, passed_b, crossed_b, home_b, [s.at[3] for s in sems])

    def put_two(out, step, left, right, dims):
        base = min(home_order[step : step + 2])
        value = dot(left[base * block : (base + 2) * block, :], right[...], dims).astype(BF)
        for i in (step, step + 1):
            at = (home_order[i] - base) * block
            out.put(i, value[at : at + block])

    for step in range(groups):
        if step % 2 == 0:
            put_two(out_a, step, att, wout, (((1,), (0,)), ((), ())))
        if step:
            out_a.middle(step - 1)
    out_a.middle(groups - 1)
    for step in range(0, groups, 2):
        project_grad(step)

    done = 0
    for h in range(heads):
        attend_back(h)
        until = min(groups, (h + 1) * ((groups + 2) // 3))
        for step in range(done, until):
            out_a.last(step)
        done = until
    for step in range(groups + 2):
        if step < groups and step % 2 == 0:
            put_two(out_b, step, dqkv, wqkv, NT)
        if 1 <= step <= groups:
            out_b.middle(step - 1)
        if step >= 2:
            out_b.last(step - 2)
    a.finish()
    b.finish()
    out_a.finish()
    back = dot(placing_back, home_a[...].reshape(slots, width))
    output[...] = (tokens[...].astype(F32) + back).astype(BF)
    out_b.finish()
    back = dot(placing_back, home_b[...].reshape(slots, width)) * gain[...]
    x = tokens[...].astype(F32)
    unit = (x - jnp.mean(x, axis=1, keepdims=True)) * scale
    back = back - jnp.mean(back, axis=1, keepdims=True) - unit * jnp.mean(back * unit, axis=1, keepdims=True)
    grad_tokens[...] = (cotangent[...].astype(F32) + scale * back).astype(BF)


def fused(tokens, gain, w_qkv, w_out, dest, track, cotangent, groups, heads):
    count, width = tokens.shape
    cap = 2 * count // groups
    rows, span = groups * cap * 4, heads * LANES
    sems = pltpu.SemaphoreType.DMA
    buf = lambda *shape: pltpu.VMEM(shape, BF)
    out = jax.ShapeDtypeStruct((count, width), BF)
    anywhere = pl.BlockSpec(memory_space=pl.ANY)
    return pl.pallas_call(
        functools.partial(fused_kernel, groups, heads),
        out_shape=(out, out),
        in_specs=[VMEM] * 5 + [anywhere] * 2,
        out_specs=(VMEM, VMEM),
        scratch_shapes=[
            buf(groups, cap, width + LANES), buf(groups, cap, width),
            buf(groups, 4, cap, width + LANES), buf(groups, 4, cap, width),
            buf(*w_qkv.shape), buf(*w_out.shape),
            buf(width, 3 * span), buf(span, width),
            buf(rows, 3 * span), buf(rows, span), buf(rows, span), buf(rows, 3 * span),
            buf(rows, LANES), pltpu.VMEM((8, rows), F32),
            buf(heads, rows, rows),
            pltpu.VMEM((LANES, rows), F32), pltpu.VMEM((LANES, rows), F32),
            buf(groups, 4, cap, width), buf(groups, 4, cap, width),
            buf(groups, 2, cap, width), buf(groups, 2, cap, width),
        ]
        + [buf(groups, cap, width)] * 8
        + [sems((2,))]
        + [sems((4, groups))] * 4
        + [sems((4, groups, 2))] * 2,
        compiler_params=pltpu.CompilerParams(
            collective_id=0, has_side_effects=True, vmem_limit_bytes=62 * 2**20
        ),
    )(tokens, cotangent, gain.reshape(1, width), dest.reshape(1, count), track.reshape(1, count), w_qkv, w_out)


def attention_kernel(tiles, query, key, value, grad, tq, tk, att, dq, dk, dv, dk_t, dv_t):
    tile = pl.program_id(1)
    q, k, v, g = query[...], key[...], value[...], grad[...]
    scores = jnp.where(tq[...] == tk[...], dot(q, k, NT) * SCALE, -1e30)
    top = jnp.max(scores, axis=1, keepdims=True)
    expo = jnp.exp(scores - top)
    prob = expo * (1.0 / jnp.sum(expo, axis=1, keepdims=True))
    weights = prob.astype(BF)
    result = dot(weights, v).astype(BF)
    att[...] = result
    delta = jnp.sum(g.astype(F32) * result.astype(F32), axis=1, keepdims=True)
    dscore = (prob * (dot(g, v, NT) - delta)).astype(BF)
    dq[...] = (dot(dscore, k) * SCALE).astype(BF)

    @pl.when(tile == 0)
    def _():
        dk_t[...] = jnp.zeros_like(dk_t)
        dv_t[...] = jnp.zeros_like(dv_t)

    dk_t[...] += dot(q, dscore, TN)
    dv_t[...] += dot(g, weights, TN)

    @pl.when(tile == tiles - 1)
    def _():
        dk[...] = (dk_t[...].T * SCALE).astype(BF)
        dv[...] = dv_t[...].T.astype(BF)


def attention(qkv, gatt, track):
    slots = qkv.shape[0]
    heads = gatt.shape[1] // LANES
    rows = min(256, slots)
    tiles = slots // rows
    whole = lambda first: pl.BlockSpec((slots, LANES), lambda h, t: (0, first + h))
    part = pl.BlockSpec((rows, LANES), lambda h, t: (t, h))
    out = jax.ShapeDtypeStruct((slots, heads * LANES), BF)
    return pl.pallas_call(
        functools.partial(attention_kernel, tiles),
        grid=(heads, tiles),
        out_shape=(out,) * 4,
        in_specs=[
            part, whole(heads), whole(2 * heads), part,
            pl.BlockSpec((rows, 1), lambda h, t: (t, 0)),
            pl.BlockSpec((1, slots), lambda h, t: (0, 0)),
        ],
        out_specs=(part, part, whole(0), whole(0)),
        scratch_shapes=[pltpu.VMEM((LANES, slots), F32), pltpu.VMEM((LANES, slots), F32)],
        compiler_params=pltpu.CompilerParams(vmem_limit_bytes=48 * 2**20),
    )(qkv, qkv, qkv, gatt, track[:, None], track[None, :])


def normalize(rows, gain):
    mean = jnp.mean(rows, axis=1, keepdims=True)
    centred = rows - mean
    var = jnp.mean(centred * centred, axis=1, keepdims=True)
    return centred * lax.rsqrt(var + 1e-06) * gain[None, :]


def local(tokens, gain, w_qkv, w_out, dest, track, cotangent):
    count, width = tokens.shape
    groups, parts = lax.axis_size("dp"), lax.axis_size("seq")
    capacity = 2 * count // groups
    slots = groups * capacity
    heads = HEADS // parts
    part = lax.axis_index("seq")
    if capacity % 16 == 0 and parts == 4 and groups <= LANES:
        return fused(tokens, gain, w_qkv, w_out, dest, track, cotangent, groups, heads)

    clip_group = dest[:, 0]
    onehot = (clip_group[:, None] == jnp.arange(groups, dtype=jnp.int32)[None, :]).astype(jnp.int32)
    rank = jnp.sum(jnp.cumsum(onehot, axis=0) * onehot, axis=1) - 1
    slot_ids = jnp.arange(slots, dtype=jnp.int32)
    placing = (clip_group * capacity + rank)[None, :] == slot_ids[:, None]
    placing_back = (clip_group * capacity + rank)[:, None] == slot_ids[None, :]

    rows_f = tokens.astype(F32)
    normed, ln_back = jax.vjp(lambda value: normalize(value, gain), rows_f)
    marks = jnp.broadcast_to((track + 1).astype(BF)[:, None], (count, LANES))
    payload = jnp.concatenate([normed.astype(BF), cotangent, marks], axis=1)
    payload = dot(placing.astype(BF), payload).astype(BF).reshape(groups, capacity, -1)

    pad = LANES - HEAD
    mine = lax.dynamic_index_in_dim(w_qkv.reshape(width, 3, parts, heads, HEAD), part, 2, keepdims=False)
    mine = jnp.pad(mine, ((0, 0), (0, 0), (0, 0), (0, pad))).reshape(width, 3 * heads * LANES)
    mine_out = lax.dynamic_index_in_dim(w_out.reshape(parts, heads, HEAD, width), part, 0, keepdims=False)
    mine_out = jnp.pad(mine_out, ((0, 0), (0, pad), (0, 0))).reshape(heads * LANES, width)
    moved = lax.all_to_all(payload.reshape(slots, -1), "dp", split_axis=0, concat_axis=0, tiled=True)
    moved = lax.all_gather(moved, "seq", axis=0, tiled=True)
    qkv = dot(moved[:, :width], mine).astype(BF)
    gatt = dot(moved[:, width : 2 * width], mine_out, NT).astype(BF)
    marked = moved[:, 2 * width :]

    att, dq, dk, dv = attention(qkv, gatt, marked[:, 0].astype(F32))

    dqkv = jnp.concatenate([dq, dk, dv], axis=1)
    sums = jnp.concatenate([dot(att, mine_out), dot(dqkv, mine, NT)], axis=1).astype(BF)
    sums = lax.all_to_all(sums.reshape(parts, slots, -1), "seq", split_axis=0, concat_axis=0, tiled=True)
    sums = jnp.sum(sums.astype(F32), axis=0).astype(BF)
    back = lax.all_to_all(sums, "dp", split_axis=0, concat_axis=0, tiled=True)

    back = dot(placing_back.astype(BF), back.reshape(slots, 2 * width))
    output = (rows_f + back[:, :width]).astype(BF)
    grad_tokens = (cotangent.astype(F32) + ln_back(back[:, width:])[0]).astype(BF)
    return (output, grad_tokens)


def solution(mesh):
    return jax.shard_map(
        local,
        mesh=mesh,
        in_specs=(
            P(("dp", "seq"), None),
            P(),
            P(),
            P(),
            P(("dp", "seq"), None),
            P(("dp", "seq")),
            P(("dp", "seq"), None),
        ),
        out_specs=(P(("dp", "seq"), None), P(("dp", "seq"), None)),
        check_vma=False,
    )
```
